256 devices in a mesh: island: 4 (over y_hi, core), fsdp: 64 (over z, x, y_lo).
Axes of the slice: x: 4, y: 4 (y_hi: 2, y_lo: 2; y = y_hi * 2 + y_lo), z: 8, core: 2. Of those that a mesh axis runs over, the one named last changes fastest.
Arguments:
- tokens: bfloat16 [4, 16384, 8192], P('island', 'fsdp'), may hold values from -6 to 6
- cotangent: bfloat16 [4, 16384, 512], P('island', 'fsdp'), may hold values from -6 to 6
- key_weight: bfloat16 [4, 8192, 512], P('island', 'fsdp'), may hold values from -0.0625 to 0.0625
- quant_codes: int32 [4, 1024, 8192], P('island', 'fsdp'), may hold values from 0 to 15
- zero_points: int32 [4, 1024, 64], P('island', 'fsdp'), may hold values from 0 to 15
- minima: float32 [4, 1024, 64], P('island', 'fsdp'), may hold values from -0.5 to 0.5
- quant_steps: float32 [4, 1024, 64], P('island', 'fsdp'), may hold values from 0.01 to 0.1
- momentum: float32 [1024, 8192], P('fsdp'), may hold values from -4 to 4
- params: float32 [1024, 8192], P('fsdp'), may hold values from -6 to 6
Outputs:
- projected: bfloat16 [4, 16384, 512], P('island', 'fsdp')
- token_grad: bfloat16 [4, 16384, 8192], P('island', 'fsdp')
- weight_grad: float32 [4, 8192, 512], P('island', 'fsdp')
- new_momentum: float32 [1024, 8192], P('fsdp')
- new_params: float32 [1024, 8192], P('fsdp')
The draws below stay inside these ranges and needn't reach their ends.
All inputs are finite; a program needn't handle non-finite values.
Results may differ from the reference program's by a relative error of at most 0.0054.
Values may be sent and summed in bfloat16 or wider, within the bound.
No kernel may reach another device: no remote copies, remote signals or barrier semaphores. Data moves between devices by JAX's collectives and lax.ppermute only.
A program may use at most 128 MiB of HBM per device.

```python
import math
import jax
import jax.numpy as jnp
from jax import lax

D = 8192
HEAD = 128
KV_HEADS = 4
GROUP = 128
ISLAND_TOK = 16384
FRAG = 1024
GROUPS = 64
N_ISLAND = 4


def place_ends(entries, key, low, top_value):
    spot = [jax.random.randint(jax.random.fold_in(key, axis), (), 0, length) for axis, length in enumerate(entries.shape)]
    main_axis = entries.shape.index(max(entries.shape))
    next_to = spot[:main_axis] + [(spot[main_axis] + 1) % entries.shape[main_axis]] + spot[main_axis + 1:]
    return entries.at[tuple(spot)].set(low).at[tuple(next_to)].set(top_value)


def levels(stream_key, dims, shards, smallest, high):
    loudness, own = 1.0, jax.random.fold_in(stream_key, 6)
    for axis_at, shards_of in shards:
        heights = jnp.exp(jax.random.uniform(jax.random.fold_in(own, axis_at), (shards_of,), jnp.float32, smallest / len(shards), high / len(shards)))
        loudness = loudness * jnp.repeat(heights, dims[axis_at] // shards_of).reshape([-1 if axis == axis_at else 1 for axis in range(len(dims))])
    return loudness


def normal_values(key, extent, scale, most, pieces=(), dtype=jnp.bfloat16):
    gain = levels(key, extent, pieces, -0.22, 0.18) if pieces else 1.0
    array = jax.random.normal(key, extent, jnp.float32) * scale * gain
    return jnp.minimum(jnp.maximum(array, -most), most).astype(dtype)


def setup_inputs(seed: int = 0) -> dict:
    seeds = jax.random.split(jax.random.key(seed), 10)
    tokens = normal_values(seeds[0], (N_ISLAND, ISLAND_TOK, D), 1.0, 6.0, ((0, 4), (1, 64)))
    cotangent = normal_values(seeds[1], (N_ISLAND, ISLAND_TOK, KV_HEADS * HEAD), 1.0, 6.0, ((0, 4), (1, 64)))
    key_weight = normal_values(seeds[2], (N_ISLAND, D, KV_HEADS * HEAD), D ** -0.5, 0.0625, ((0, 4), (1, 64)))
    quant_codes = place_ends(jax.random.randint(seeds[3], (N_ISLAND, FRAG, D), 0, 16), jax.random.fold_in(seeds[3], 1), 0, 15).astype(jnp.int32)
    zero_points = place_ends(jax.random.randint(seeds[4], (N_ISLAND, FRAG, GROUPS), 0, 16), jax.random.fold_in(seeds[4], 1), 0, 15).astype(jnp.int32)
    minima = jnp.clip(jax.random.uniform(seeds[5], (N_ISLAND, FRAG, GROUPS), jnp.float32, -0.5, 0.5) * levels(seeds[5], (N_ISLAND, FRAG, GROUPS), ((0, 4), (1, 64)), -0.4, 0.0), -0.5, 0.5)
    quant_steps = jnp.clip(jnp.exp(math.log(0.1) - 2.3025851 * jax.random.uniform(seeds[6], (N_ISLAND, FRAG, GROUPS), jnp.float32) ** levels(seeds[6], (N_ISLAND, FRAG, GROUPS), ((0, 4), (1, 64)), -0.2, 0.2)), 0.01, 0.1)
    momentum = normal_values(seeds[7], (FRAG, D), 0.5, 4.0, ((0, 64),), jnp.float32)
    params = normal_values(seeds[8], (FRAG, D), 1.0, 6.0, ((0, 64),), jnp.float32)
    return {"tokens": tokens, "cotangent": cotangent, "key_weight": key_weight, "quant_codes": quant_codes, "zero_points": zero_points, "minima": minima, "quant_steps": quant_steps, "momentum": momentum, "params": params}


def dequantize(quant_codes, zero_points, minima, quant_steps):
    shape = quant_codes.shape
    grouped = quant_codes.reshape(shape[:-1] + (shape[-1] // GROUP, GROUP))
    offset = (grouped - zero_points[..., None]).astype(jnp.float32)
    values = quant_steps[..., None] * offset + minima[..., None]
    return values.reshape(shape)

def island_step(block):
    inputs, cot_rows, weight = block
    keys = jnp.dot(inputs, weight, preferred_element_type=jnp.float32).astype(jnp.bfloat16)
    back = jnp.dot(cot_rows, weight.T, preferred_element_type=jnp.float32).astype(jnp.bfloat16)
    grad = jnp.dot(inputs.T, cot_rows, preferred_element_type=jnp.float32) * (1.0 / math.sqrt(ISLAND_TOK))
    return (keys, back, grad)

def reference(tokens, cotangent, key_weight, quant_codes, zero_points, minima, quant_steps, momentum, params):
    projected, token_grad, weight_grad = lax.map(island_step, (tokens, cotangent, key_weight))
    values = dequantize(quant_codes, zero_points, minima, quant_steps)
    delta = lax.optimization_barrier(jnp.sum(values, axis=0)) / N_ISLAND
    new_momentum = 0.9 * momentum + delta
    new_params = params - 0.7 * (delta + 0.9 * new_momentum)
    return (projected, token_grad, weight_grad, new_momentum, new_params)
```

```python
import math

import jax
import jax.numpy as jnp
from jax import lax
from jax.sharding import Mesh
from jax.sharding import PartitionSpec as P

GROUP = 128
Z, X, Y = 8, 4, 2
F32, BF16 = jnp.float32, jnp.bfloat16


def dequantize(quant_codes, zero_points, minima, quant_steps):
    shape = quant_codes.shape
    grouped = quant_codes.reshape(shape[:-1] + (shape[-1] // GROUP, GROUP))
    offset = (grouped - zero_points[..., None]).astype(F32)
    values = quant_steps[..., None] * offset + minima[..., None]
    return values.reshape(shape)


def shift(block, axis, by):
    size = lax.axis_size(axis)
    return lax.ppermute(block, axis, [(i, (i + by) % size) for i in range(size)])


def pick(pieces, index):
    result = pieces[0]
    for k in range(1, len(pieces)):
        result = jnp.where(index == k, pieces[k], result)
    return result


def outer_step(quant_codes, zero_points, minima, quant_steps, momentum, params):
    values = dequantize(quant_codes, zero_points, minima, quant_steps).astype(BF16)
    core = shift(values, "c", 1)
    far = shift(values, "yh", 1)
    far_core = lax.ppermute(values, ("yh", "c"), [(i, 3 - i) for i in range(4)])
    summed = (values.astype(F32) + core.astype(F32)) + (far.astype(F32) + far_core.astype(F32))
    delta = summed / 4
    new_momentum = 0.9 * momentum + delta
    new_params = params - 0.7 * (delta + 0.9 * new_momentum)
    return new_momentum, new_params


def gather_z(block, z):
    prev, succ = shift(block, "z", 1), shift(block, "z", -1)
    prev2 = shift(jnp.stack([block, prev]), "z", 2)
    succ2 = shift(jnp.stack([block, succ]), "z", -2)
    half = block.shape[0] // 2
    far = jnp.concatenate([shift(prev2[1][:half], "z", 1), shift(succ2[1][half:], "z", -1)])
    ring = [block, succ, succ2[0], succ2[1], far, prev2[1], prev2[0], prev]
    return jnp.stack([pick(ring, (j - z) % Z) for j in range(Z)])


def scatter_z(blocks, z):
    def at(k):
        return lax.dynamic_index_in_dim(blocks, (z + k) % Z, 0, keepdims=False)

    half = blocks.shape[1] // 2
    far = at(4).astype(BF16)
    up, down = shift(far[:half], "z", 1), shift(far[half:], "z", -1)
    third = jnp.concatenate([at(3)[:half] + up.astype(F32), at(3)[half:]])
    third_back = jnp.concatenate([at(-3)[:half], at(-3)[half:] + down.astype(F32)])
    up = shift(jnp.stack([at(2), third]).astype(BF16), "z", 2).astype(F32)
    down = shift(jnp.stack([at(-2), third_back]).astype(BF16), "z", -2).astype(F32)
    up1 = shift((at(1) + up[1]).astype(BF16), "z", 1).astype(F32)
    down1 = shift((at(-1) + down[1]).astype(BF16), "z", -1).astype(F32)
    return (at(0) + up[0] + down[0]) + (up1 + down1)


def local(
    tokens, cotangent, key_weight, quant_codes, zero_points, minima, quant_steps, momentum, params
):
    tokens, cot, weight = tokens[0], cotangent[0], key_weight[0]
    rows, width = tokens.shape
    heads = cot.shape[1]
    part = weight.shape[0]
    scaling = 1.0 / math.sqrt(rows * Z * X * Y)
    z, x, y = lax.axis_index("z"), lax.axis_index("x"), lax.axis_index("yl")
    split = tokens.reshape(rows, Z, X, Y, part)
    tokens_a = split[:, :, :, 0].reshape(rows, width // 2)
    tokens_b = split[:, :, :, 1]

    other = shift(weight, "yl", 1)
    weight_a = jnp.where(y == 0, weight, other)
    weight_b = jnp.where(y == 0, other, weight)

    grad_a = lax.dot_general(
        tokens_a, cot, (((0,), (0,)), ((), ())), preferred_element_type=F32
    ).astype(BF16)
    grad_a = lax.psum_scatter(grad_a, "z", scatter_dimension=0, tiled=True)

    ring = [weight_a] + [shift(weight_a, "x", k) for k in range(1, X)]
    weight_a = jnp.concatenate([pick(ring, (x - j) % X) for j in range(X)])
    weight_a = lax.all_gather(weight_a, "z", axis=0, tiled=True)

    def chunk(k):
        mine = lax.dynamic_index_in_dim(tokens_b, (x + k) % X, 2, keepdims=False)
        return lax.dot_general(
            mine.reshape(rows, Z * part),
            cot,
            (((0,), (0,)), ((), ())),
            preferred_element_type=F32,
        )

    half = Z * part // 2
    far, ahead, behind, own = chunk(2), chunk(1), chunk(-1), chunk(0)
    up = shift(jnp.concatenate([far[:half], ahead[half:]]).astype(BF16), "x", 1).astype(F32)
    down = shift(jnp.concatenate([behind[:half], far[half:]]).astype(BF16), "x", -1).astype(F32)
    up1 = shift((ahead[:half] + up[:half]).astype(BF16), "x", 1).astype(F32)
    down1 = shift((behind[half:] + down[half:]).astype(BF16), "x", -1).astype(F32)
    grad_b = jnp.concatenate(
        [own[:half] + (up1 + down[:half]), own[half:] + (down1 + up[half:])]
    ).reshape(Z, part, heads)

    weight_b = gather_z(weight_b, z)
    up = shift(weight_b, "x", 1)
    down = shift(weight_b, "x", -1)
    far = jnp.concatenate([shift(up[: Z // 2], "x", 1), shift(down[Z // 2 :], "x", -1)])
    whole_b = jnp.zeros((Z, X, part, heads), BF16)
    for k, piece in ((0, weight_b), (-1, up), (1, down), (2, far)):
        whole_b = lax.dynamic_update_slice(whole_b, piece[:, None], (0, (x + k) % X, 0, 0))
    weight_b = whole_b.reshape(width // 2, heads)

    grad_b = scatter_z(grad_b, z)

    over_x = grad_a.reshape(X, part, heads)

    def at(k):
        return lax.dynamic_index_in_dim(over_x, (x + k) % X, 0, keepdims=False)

    grad_a = at(0).astype(F32)
    for k in range(1, X):
        grad_a = grad_a + shift(at(k), "x", k).astype(F32)

    theirs = jnp.where(y == 0, grad_b, grad_a).astype(BF16)
    mine = jnp.where(y == 0, grad_a, grad_b)
    weight_grad = (mine + shift(theirs, "yl", 1).astype(F32)) * scaling

    def back(piece):
        part_grad = lax.dot_general(
            cot, piece, (((1,), (1,)), ((), ())), preferred_element_type=F32
        )
        return part_grad.astype(BF16).reshape(rows, Z * X, 1, part)

    tokens_b = tokens_b.reshape(rows, width // 2)
    projected = jnp.dot(tokens_b, weight_b, preferred_element_type=F32)
    projected = projected + jnp.dot(tokens_a, weight_a, preferred_element_type=F32)
    token_grad = jnp.concatenate([back(weight_a), back(weight_b)], axis=2).reshape(rows, width)

    new_momentum, new_params = outer_step(
        quant_codes[0], zero_points[0], minima[0], quant_steps[0], momentum, params
    )
    return (
        projected.astype(BF16)[None],
        token_grad[None],
        weight_grad[None],
        new_momentum,
        new_params,
    )


def solution(mesh):
    fine = Mesh(mesh.devices.reshape(2, 2, Z, X, Y), ("yh", "c", "z", "x", "yl"))
    island, fsdp = ("yh", "c"), ("z", "x", "yl")
    whole = P(island, fsdp, None)
    return jax.shard_map(
        local,
        mesh=fine,
        in_specs=(whole,) * 7 + (P(fsdp, None),) * 2,
        out_specs=(whole,) * 3 + (P(fsdp, None),) * 2,
        check_vma=False,
    )
```

```python
import math

import jax
import jax.numpy as jnp
from jax import lax
from jax.experimental import pallas as pl
from jax.experimental.pallas import tpu as pltpu
from jax.sharding import Mesh
from jax.sharding import PartitionSpec as P

GROUP = 128
Z, X, Y = 8, 4, 2
WEIGHT_SPLIT = 256
GRAD_SPLIT = 384
F32, BF16 = jnp.float32, jnp.bfloat16
VMEM_LIMIT = 56 * 1024 * 1024


def dequantize(quant_codes, zero_points, minima, quant_steps):
    shape = quant_codes.shape
    grouped = quant_codes.reshape(shape[:-1] + (shape[-1] // GROUP, GROUP))
    offset = (grouped - zero_points[..., None]).astype(F32)
    values = quant_steps[..., None] * offset + minima[..., None]
    return values.reshape(shape)


def shift(block, axis, by):
    size = lax.axis_size(axis)
    return lax.ppermute(block, axis, [(i, (i + by) % size) for i in range(size)])


def after(value, *earlier):
    return lax.optimization_barrier((value, *earlier))[0]


def outer_values(quant_codes, zero_points, minima, quant_steps):
    values = dequantize(quant_codes, zero_points, minima, quant_steps).astype(BF16)
    core = shift(values, "c", 1)
    far = shift(values, "yh", 1)
    far_core = lax.ppermute(values, ("yh", "c"), [(i, 3 - i) for i in range(4)])
    return values, core, far, far_core


def outer_step(exchanged, momentum, params):
    values, core, far, far_core = (v.astype(F32) for v in exchanged)
    delta = ((values + core) + (far + far_core)) / 4
    new_momentum = 0.9 * momentum + delta
    new_params = params - 0.7 * (delta + 0.9 * new_momentum)
    return new_momentum, new_params


def grad_kernel(
    place, tokens, cot, grad_a, keep, send, columns, cot_rows, cot_turned, a, kept, sent, sems
):
    part = kept.shape[3]
    load = pltpu.make_async_copy(cot, cot_rows, sems.at[0, Z])
    load.start()
    loads = []
    for j in range(Z):
        width = columns.shape[2]
        at = pl.multiple_of(lax.rem(place[0] + j, Z) * width, width)
        loads.append(
            pltpu.make_async_copy(tokens.at[:, pl.ds(at, width)], columns.at[j], sems.at[0, j])
        )
        loads[j].start()
    load.wait()
    cot_turned[...] = cot_rows[...].T
    first = place[2] == 0
    stores = []
    for j in range(Z):
        loads[j].wait()
        for k in range(X):
            grad = jnp.dot(
                cot_turned[...],
                columns[j, :, k * Y * part : (k + 1) * Y * part],
                preferred_element_type=F32,
            ).astype(BF16)
            a[j, k] = grad[:GRAD_SPLIT]
            lower, upper = grad[GRAD_SPLIT:, :part], grad[GRAD_SPLIT:, part:]
            kept[j, k] = jnp.where(first, lower, upper)
            sent[j, k] = jnp.where(first, upper, lower)
        own = lax.rem(place[0] + j, Z)
        for i, (buffer, out, to) in enumerate(((a, grad_a, j), (kept, keep, own), (sent, send, own))):
            store = pltpu.make_async_copy(buffer.at[j], out.at[:, to], sems.at[1 + i, j])
            store.start()
            stores.append(store)
    for store in stores:
        store.wait()


def gradients(place, tokens, cot, part):
    rows, width = tokens.shape
    heads = cot.shape[1]
    anywhere = pl.BlockSpec(memory_space=pl.ANY)
    shapes = [(GRAD_SPLIT, Y * part), (heads - GRAD_SPLIT, part), (heads - GRAD_SPLIT, part)]
    return pl.pallas_call(
        grad_kernel,
        in_specs=[pl.BlockSpec(memory_space=pltpu.SMEM), anywhere, anywhere],
        out_specs=[anywhere] * 3,
        out_shape=[jax.ShapeDtypeStruct((X, Z) + shape, BF16) for shape in shapes],
        scratch_shapes=[
            pltpu.VMEM((Z, rows, width // Z), BF16),
            pltpu.VMEM((rows, heads), BF16),
            pltpu.VMEM((heads, rows), BF16),
        ]
        + [pltpu.VMEM((Z, X) + shape, BF16) for shape in shapes]
        + [pltpu.SemaphoreType.DMA((4, Z + 1))],
        compiler_params=pltpu.CompilerParams(vmem_limit_bytes=VMEM_LIMIT),
        cost_estimate=pl.CostEstimate(
            flops=2 * rows * width * heads,
            bytes_accessed=2 * width * (rows + heads),
            transcendentals=0,
        ),
    )(place, tokens, cot)


def product_kernel(place, tokens, cot, weight_a, weight_c, other_c, keys, back, total):
    j = pl.program_id(0)
    part = weight_c.shape[2]
    first = place[2] == 0
    added = None
    for k in range(X):
        columns = slice(k * Y * part, (k + 1) * Y * part)
        at = lax.rem(k - place[1] + X, X)
        mine, theirs = weight_c[0, at], other_c[0, at]
        right = jnp.concatenate(
            [jnp.where(first, mine, theirs), jnp.where(first, theirs, mine)], axis=0
        )
        weight = jnp.concatenate([weight_a[0, at], right], axis=1)
        product = jnp.dot(tokens[:, columns], weight, preferred_element_type=F32)
        added = product if added is None else added + product
        back[:, columns] = lax.dot_general(
            cot[...], weight, (((1,), (1,)), ((), ())), preferred_element_type=F32
        ).astype(BF16)

    @pl.when(j == 0)
    def _():
        total[...] = added

    @pl.when(j > 0)
    def _():
        total[...] += added

    @pl.when(j == Z - 1)
    def _():
        keys[...] = total[...].astype(BF16)


def products(place, tokens, cot, weight_a, weight_c, other_c):
    rows, width = tokens.shape
    heads = cot.shape[1]
    part = weight_c.shape[2]
    by_z = lambda j, place: (j, 0, 0, 0)
    return pl.pallas_call(
        product_kernel,
        grid_spec=pltpu.PrefetchScalarGridSpec(
            num_scalar_prefetch=1,
            grid=(Z,),
            in_specs=[
                pl.BlockSpec((rows, width // Z), lambda j, place: (0, j)),
                pl.BlockSpec((rows, heads), lambda j, place: (0, 0)),
                pl.BlockSpec((1, X, Y * part, WEIGHT_SPLIT), by_z),
                pl.BlockSpec((1, X, part, heads - WEIGHT_SPLIT), by_z),
                pl.BlockSpec((1, X, part, heads - WEIGHT_SPLIT), by_z),
            ],
            out_specs=[
                pl.BlockSpec((rows, heads), lambda j, place: (0, 0)),
                pl.BlockSpec((rows, width // Z), lambda j, place: (0, j)),
            ],
            scratch_shapes=[pltpu.VMEM((rows, heads), F32)],
        ),
        out_shape=[
            jax.ShapeDtypeStruct((rows, heads), BF16),
            jax.ShapeDtypeStruct((rows, width), BF16),
        ],
        compiler_params=pltpu.CompilerParams(vmem_limit_bytes=VMEM_LIMIT),
        cost_estimate=pl.CostEstimate(
            flops=4 * rows * width * heads,
            bytes_accessed=4 * width * (rows + heads // 2),
            transcendentals=0,
        ),
    )(place, tokens, cot, weight_a, weight_c, other_c)


def gather_x(block):
    return jnp.stack([block] + [shift(block, "x", -k) for k in range(1, X)])


def local(
    tokens, cotangent, key_weight, quant_codes, zero_points, minima, quant_steps, momentum, params
):
    tokens, cot, weight = tokens[0], cotangent[0], key_weight[0]
    rows, width = tokens.shape
    part = weight.shape[0]
    scaling = 1.0 / math.sqrt(rows * Z * X * Y)
    z, x, y = lax.axis_index("z"), lax.axis_index("x"), lax.axis_index("yl")
    place = jnp.stack([z, x, y]).astype(jnp.int32)

    lower = weight[:, :WEIGHT_SPLIT]
    upper = shift(lower, "yl", 1)
    weight_c = gather_x(weight[:, WEIGHT_SPLIT:])
    weight_c, upper = lax.optimization_barrier((weight_c, upper))
    place = after(place, weight_c)
    weight_c = lax.all_gather(weight_c, "z")
    grad_a, keep, send = gradients(place, tokens, cot, part)

    grad_a = lax.psum_scatter(grad_a, "x", scatter_dimension=0, tiled=True)[0]
    got = shift(send, "yl", 1)
    upper = after(upper, send)
    weight_a = jnp.concatenate(
        [jnp.where(y == 0, lower, upper), jnp.where(y == 0, upper, lower)], axis=0
    )
    weight_a = gather_x(weight_a)

    got = after(got, weight_a)
    grad_c = (keep.astype(F32) + got.astype(F32)).astype(BF16)
    grad_c_x = lax.psum_scatter(grad_c, "x", scatter_dimension=0, tiled=True)[0]

    weight_c = after(weight_c, grad_c)
    weight_a = lax.all_gather(after(weight_a, weight_c), "z")
    other_c = shift(weight_c, "yl", 1)

    quant_codes = after(quant_codes[0], weight_c)
    exchanged = outer_values(quant_codes, zero_points[0], minima[0], quant_steps[0])
    new_momentum, new_params = outer_step(exchanged, momentum, params)

    grad_a = after(grad_a, new_params)
    half = GRAD_SPLIT // 2
    at = grad_a.astype(F32)
    up, down = shift(grad_a[4][:half], "z", 1), shift(grad_a[4][half:], "z", -1)
    up = jnp.concatenate([at[3][:half] + up.astype(F32), at[3][half:]]).astype(BF16)
    down = jnp.concatenate([at[5][:half], at[5][half:] + down.astype(F32)]).astype(BF16)
    up, down = shift(up, "z", 1), shift(down, "z", -1)
    up, down = (at[2] + up.astype(F32)).astype(BF16), (at[6] + down.astype(F32)).astype(BF16)
    grad_c = lax.all_to_all(after(grad_c_x, up), "z", 0, 0, tiled=True)
    up, down = shift(up, "z", 1), shift(down, "z", -1)
    up, down = (at[1] + up.astype(F32)).astype(BF16), (at[7] + down.astype(F32)).astype(BF16)
    keys, back = products(place, tokens, cot, weight_a, weight_c, other_c)
    up, down = after(up, keys, grad_c), after(down, keys, grad_c)
    up, down = shift(up, "z", 1), shift(down, "z", -1)
    grad_a = at[0] + (up.astype(F32) + down.astype(F32))
    lower, upper = grad_a[:, :part], grad_a[:, part:]
    theirs = jnp.where(y == 0, upper, lower).astype(BF16)
    mine = jnp.where(y == 0, lower, upper)
    grad_a = mine + shift(theirs, "yl", 1).astype(F32)
    grad_c = jnp.sum(grad_c.astype(F32), axis=0)
    weight_grad = jnp.concatenate([grad_a, grad_c]).T * scaling

    return keys[None], back[None], weight_grad[None], new_momentum, new_params


def solution(mesh):
    fine = Mesh(mesh.devices.reshape(2, 2, Z, X, Y), ("yh", "c", "z", "x", "yl"))
    island, fsdp = ("yh", "c"), ("z", "x", "yl")
    whole = P(island, fsdp, None)
    return jax.shard_map(
        local,
        mesh=fine,
        in_specs=(whole,) * 7 + (P(fsdp, None),) * 2,
        out_specs=(whole,) * 3 + (P(fsdp, None),) * 2,
        check_vma=False,
    )
```

```python
import math

import jax
import jax.numpy as jnp
from jax import lax
from jax.experimental import pallas as pl
from jax.experimental.pallas import tpu as pltpu
from jax.sharding import Mesh
from jax.sharding import PartitionSpec as P

GROUP = 128
Z, X, Y = 8, 4, 2
WEIGHT_SPLIT = 256
GRAD_SPLIT = 320
F32, BF16 = jnp.float32, jnp.bfloat16
VMEM_LIMIT = 56 * 1024 * 1024


def dequantize(quant_codes, zero_points, minima, quant_steps):
    shape = quant_codes.shape
    grouped = quant_codes.reshape(shape[:-1] + (shape[-1] // GROUP, GROUP))
    offset = (grouped - zero_points[..., None]).astype(F32)
    values = quant_steps[..., None] * offset + minima[..., None]
    return values.reshape(shape)


def shift(block, axis, by):
    size = lax.axis_size(axis)
    return lax.ppermute(block, axis, [(i, (i + by) % size) for i in range(size)])


def after(value, *earlier):
    return lax.optimization_barrier((value, *earlier))[0]


def outer_values(quant_codes, zero_points, minima, quant_steps):
    values = dequantize(quant_codes, zero_points, minima, quant_steps).astype(BF16)
    core = shift(values, "c", 1)
    far = shift(values, "yh", 1)
    far_core = lax.ppermute(values, ("yh", "c"), [(i, 3 - i) for i in range(4)])
    return values, core, far, far_core


def outer_step(exchanged, momentum, params):
    values, core, far, far_core = (v.astype(F32) for v in exchanged)
    delta = ((values + core) + (far + far_core)) / 4
    new_momentum = 0.9 * momentum + delta
    new_params = params - 0.7 * (delta + 0.9 * new_momentum)
    return new_momentum, new_params


def grad_kernel(
    place, tokens, cot, grad_a, keep, send, columns, cot_rows, cot_turned, a, kept, sent, sems
):
    part = kept.shape[3]
    load = pltpu.make_async_copy(cot, cot_rows, sems.at[0, Z])
    load.start()
    loads = []
    for j in range(Z):
        width = columns.shape[2]
        at = pl.multiple_of(lax.rem(place[0] + j, Z) * width, width)
        loads.append(
            pltpu.make_async_copy(tokens.at[:, pl.ds(at, width)], columns.at[j], sems.at[0, j])
        )
        loads[j].start()
    load.wait()
    cot_turned[...] = cot_rows[...].T
    first = place[2] == 0
    stores = []
    for j in range(Z):
        loads[j].wait()
        for k in range(X):
            grad = jnp.dot(
                cot_turned[...],
                columns[j, :, k * Y * part : (k + 1) * Y * part],
                preferred_element_type=F32,
            ).astype(BF16)
            a[j, k] = grad[:GRAD_SPLIT]
            lower, upper = grad[GRAD_SPLIT:, :part], grad[GRAD_SPLIT:, part:]
            kept[j, k] = jnp.where(first, lower, upper)
            sent[j, k] = jnp.where(first, upper, lower)
        own = lax.rem(place[0] + j, Z)
        for i, (buffer, out, to) in enumerate(((a, grad_a, j), (kept, keep, own), (sent, send, own))):
            store = pltpu.make_async_copy(buffer.at[j], out.at[:, to], sems.at[1 + i, j])
            store.start()
            stores.append(store)
    for store in stores:
        store.wait()


def gradients(place, tokens, cot, part):
    rows, width = tokens.shape
    heads = cot.shape[1]
    anywhere = pl.BlockSpec(memory_space=pl.ANY)
    shapes = [(GRAD_SPLIT, Y * part), (heads - GRAD_SPLIT, part), (heads - GRAD_SPLIT, part)]
    return pl.pallas_call(
        grad_kernel,
        in_specs=[pl.BlockSpec(memory_space=pltpu.SMEM), anywhere, anywhere],
        out_specs=[anywhere] * 3,
        out_shape=[jax.ShapeDtypeStruct((X, Z) + shape, BF16) for shape in shapes],
        scratch_shapes=[
            pltpu.VMEM((Z, rows, width // Z), BF16),
            pltpu.VMEM((rows, heads), BF16),
            pltpu.VMEM((heads, rows), BF16),
        ]
        + [pltpu.VMEM((Z, X) + shape, BF16) for shape in shapes]
        + [pltpu.SemaphoreType.DMA((4, Z + 1))],
        compiler_params=pltpu.CompilerParams(vmem_limit_bytes=VMEM_LIMIT),
        cost_estimate=pl.CostEstimate(
            flops=2 * rows * width * heads,
            bytes_accessed=2 * width * (rows + heads),
            transcendentals=0,
        ),
    )(place, tokens, cot)


def product_kernel(place, tokens, cot, weight_a, weight_c, other_c, keys, back, total):
    j = pl.program_id(0)
    part = weight_c.shape[2]
    first = place[2] == 0
    added = None
    for k in range(X):
        columns = slice(k * Y * part, (k + 1) * Y * part)
        at = lax.rem(k - place[1] + X, X)
        mine, theirs = weight_c[0, at], other_c[0, at]
        right = jnp.concatenate(
            [jnp.where(first, mine, theirs), jnp.where(first, theirs, mine)], axis=0
        )
        weight = jnp.concatenate([weight_a[0, at], right], axis=1)
        product = jnp.dot(tokens[:, columns], weight, preferred_element_type=F32)
        added = product if added is None else added + product
        back[:, columns] = lax.dot_general(
            cot[...], weight, (((1,), (1,)), ((), ())), preferred_element_type=F32
        ).astype(BF16)

    @pl.when(j == 0)
    def _():
        total[...] = added

    @pl.when(j > 0)
    def _():
        total[...] += added

    @pl.when(j == Z - 1)
    def _():
        keys[...] = total[...].astype(BF16)


def products(place, tokens, cot, weight_a, weight_c, other_c):
    rows, width = tokens.shape
    heads = cot.shape[1]
    part = weight_c.shape[2]
    by_z = lambda j, place: (j, 0, 0, 0)
    return pl.pallas_call(
        product_kernel,
        grid_spec=pltpu.PrefetchScalarGridSpec(
            num_scalar_prefetch=1,
            grid=(Z,),
            in_specs=[
                pl.BlockSpec((rows, width // Z), lambda j, place: (0, j)),
                pl.BlockSpec((rows, heads), lambda j, place: (0, 0)),
                pl.BlockSpec((1, X, Y * part, WEIGHT_SPLIT), by_z),
                pl.BlockSpec((1, X, part, heads - WEIGHT_SPLIT), by_z),
                pl.BlockSpec((1, X, part, heads - WEIGHT_SPLIT), by_z),
            ],
            out_specs=[
                pl.BlockSpec((rows, heads), lambda j, place: (0, 0)),
                pl.BlockSpec((rows, width // Z), lambda j, place: (0, j)),
            ],
            scratch_shapes=[pltpu.VMEM((rows, heads), F32)],
        ),
        out_shape=[
            jax.ShapeDtypeStruct((rows, heads), BF16),
            jax.ShapeDtypeStruct((rows, width), BF16),
        ],
        compiler_params=pltpu.CompilerParams(vmem_limit_bytes=VMEM_LIMIT),
        cost_estimate=pl.CostEstimate(
            flops=4 * rows * width * heads,
            bytes_accessed=4 * width * (rows + heads // 2),
            transcendentals=0,
        ),
    )(place, tokens, cot, weight_a, weight_c, other_c)


def gather_x(block):
    return jnp.stack([block] + [shift(block, "x", -k) for k in range(1, X)])


def local(
    tokens, cotangent, key_weight, quant_codes, zero_points, minima, quant_steps, momentum, params
):
    tokens, cot, weight = tokens[0], cotangent[0], key_weight[0]
    rows, width = tokens.shape
    part = weight.shape[0]
    scaling = 1.0 / math.sqrt(rows * Z * X * Y)
    z, x, y = lax.axis_index("z"), lax.axis_index("x"), lax.axis_index("yl")
    place = jnp.stack([z, x, y]).astype(jnp.int32)

    lower = weight[:, :WEIGHT_SPLIT]
    upper = shift(lower, "yl", 1)
    weight_c = gather_x(weight[:, WEIGHT_SPLIT:])
    weight_c, upper = lax.optimization_barrier((weight_c, upper))
    place = after(place, weight_c)
    weight_c = lax.all_gather(weight_c, "z")
    grad_a, keep, send = gradients(place, tokens, cot, part)

    grad_a = lax.psum_scatter(grad_a, "x", scatter_dimension=0, tiled=True)[0]
    got = shift(send, "yl", 1)
    upper = after(upper, send)
    weight_a = jnp.concatenate(
        [jnp.where(y == 0, lower, upper), jnp.where(y == 0, upper, lower)], axis=0
    )
    weight_a = gather_x(weight_a)

    got = after(got, weight_a)
    grad_c = (keep.astype(F32) + got.astype(F32)).astype(BF16)
    grad_c_x = lax.psum_scatter(grad_c, "x", scatter_dimension=0, tiled=True)[0]

    weight_c = after(weight_c, grad_c)
    weight_a = lax.all_gather(after(weight_a, weight_c), "z")
    other_c = shift(weight_c, "yl", 1)

    quant_codes = after(quant_codes[0], weight_c)
    exchanged = outer_values(quant_codes, zero_points[0], minima[0], quant_steps[0])
    new_momentum, new_params = outer_step(exchanged, momentum, params)

    grad_a = after(grad_a, new_params)
    half = GRAD_SPLIT // 2
    at = grad_a.astype(F32)
    up, down = shift(grad_a[4][:half], "z", 1), shift(grad_a[4][half:], "z", -1)
    up = jnp.concatenate([at[3][:half] + up.astype(F32), at[3][half:]]).astype(BF16)
    down = jnp.concatenate([at[5][:half], at[5][half:] + down.astype(F32)]).astype(BF16)
    up, down = lax.optimization_barrier((up, down))
    up, down = shift(up, "z", 1), shift(down, "z", -1)
    up, down = (at[2] + up.astype(F32)).astype(BF16), (at[6] + down.astype(F32)).astype(BF16)
    up, down = lax.optimization_barrier((up, down))
    up, down = shift(up, "z", 1), shift(down, "z", -1)
    up, down = (at[1] + up.astype(F32)).astype(BF16), (at[7] + down.astype(F32)).astype(BF16)
    up, down = lax.optimization_barrier((up, down))
    grad_c = lax.all_to_all(after(grad_c_x, up, other_c), "z", 0, 0, tiled=True)
    up, down = shift(up, "z", 1), shift(down, "z", -1)
    grad_a = at[0] + (up.astype(F32) + down.astype(F32))
    lower, upper = grad_a[:, :part], grad_a[:, part:]
    theirs = jnp.where(y == 0, upper, lower).astype(BF16)
    mine = jnp.where(y == 0, lower, upper)
    weight_a = after(weight_a, theirs)
    grad_a = mine + shift(theirs, "yl", 1).astype(F32)
    grad_c = jnp.sum(grad_c.astype(F32), axis=0)
    weight_grad = jnp.concatenate([grad_a, grad_c]).T * scaling

    keys, back = products(place, tokens, cot, weight_a, weight_c, other_c)
    return keys[None], back[None], weight_grad[None], new_momentum, new_params


def solution(mesh):
    fine = Mesh(mesh.devices.reshape(2, 2, Z, X, Y), ("yh", "c", "z", "x", "yl"))
    island, fsdp = ("yh", "c"), ("z", "x", "yl")
    whole = P(island, fsdp, None)
    return jax.shard_map(
        local,
        mesh=fine,
        in_specs=(whole,) * 7 + (P(fsdp, None),) * 2,
        out_specs=(whole,) * 3 + (P(fsdp, None),) * 2,
        check_vma=False,
    )
```

```python
import math

import jax
import jax.numpy as jnp
from jax import lax
from jax.experimental import pallas as pl
from jax.experimental.pallas import tpu as pltpu
from jax.sharding import Mesh
from jax.sharding import PartitionSpec as P

GROUP = 128
Z, X, Y = 8, 4, 2
WEIGHT_SPLIT = 256
GRAD_SPLIT = 320
F32, BF16 = jnp.float32, jnp.bfloat16
VMEM_LIMIT = 56 * 1024 * 1024


def dequantize(quant_codes, zero_points, minima, quant_steps):
    shape = quant_codes.shape
    grouped = quant_codes.reshape(shape[:-1] + (shape[-1] // GROUP, GROUP))
    offset = (grouped - zero_points[..., None]).astype(F32)
    values = quant_steps[..., None] * offset + minima[..., None]
    return values.reshape(shape)


def shift(block, axis, by):
    size = lax.axis_size(axis)
    return lax.ppermute(block, axis, [(i, (i + by) % size) for i in range(size)])


def after(value, *earlier):
    return lax.optimization_barrier((value, *earlier))[0]


def outer_values(quant_codes, zero_points, minima, quant_steps):
    values = dequantize(quant_codes, zero_points, minima, quant_steps).astype(BF16)
    core = shift(values, "c", 1)
    far = shift(values, "yh", 1)
    far_core = lax.ppermute(values, ("yh", "c"), [(i, 3 - i) for i in range(4)])
    return values, core, far, far_core


def outer_step(exchanged, momentum, params):
    values, core, far, far_core = (v.astype(F32) for v in exchanged)
    delta = ((values + core) + (far + far_core)) / 4
    new_momentum = 0.9 * momentum + delta
    new_params = params - 0.7 * (delta + 0.9 * new_momentum)
    return new_momentum, new_params


def grad_kernel(
    place, tokens, cot, grad_a, keep, send, columns, cot_rows, cot_turned, a, kept, sent, sems
):
    part = kept.shape[3]
    load = pltpu.make_async_copy(cot, cot_rows, sems.at[0, Z])
    load.start()
    loads = []
    for j in range(Z):
        width = columns.shape[2]
        at = pl.multiple_of(lax.rem(place[0] + j, Z) * width, width)
        loads.append(
            pltpu.make_async_copy(tokens.at[:, pl.ds(at, width)], columns.at[j], sems.at[0, j])
        )
        loads[j].start()
    load.wait()
    cot_turned[...] = cot_rows[...].T
    first = place[2] == 0
    stores = []
    for j in range(Z):
        loads[j].wait()
        for k in range(X):
            grad = jnp.dot(
                cot_turned[...],
                columns[j, :, k * Y * part : (k + 1) * Y * part],
                preferred_element_type=F32,
            ).astype(BF16)
            a[j, k] = grad[:GRAD_SPLIT]
            lower, upper = grad[GRAD_SPLIT:, :part], grad[GRAD_SPLIT:, part:]
            kept[j, k] = jnp.where(first, lower, upper)
            sent[j, k] = jnp.where(first, upper, lower)
        own = lax.rem(place[0] + j, Z)
        for i, (buffer, out, to) in enumerate(((a, grad_a, j), (kept, keep, own), (sent, send, own))):
            store = pltpu.make_async_copy(buffer.at[j], out.at[:, to], sems.at[1 + i, j])
            store.start()
            stores.append(store)
    for store in stores:
        store.wait()


def gradients(place, tokens, cot, part):
    rows, width = tokens.shape
    heads = cot.shape[1]
    anywhere = pl.BlockSpec(memory_space=pl.ANY)
    shapes = [(GRAD_SPLIT, Y * part), (heads - GRAD_SPLIT, part), (heads - GRAD_SPLIT, part)]
    return pl.pallas_call(
        grad_kernel,
        in_specs=[pl.BlockSpec(memory_space=pltpu.SMEM), anywhere, anywhere],
        out_specs=[anywhere] * 3,
        out_shape=[jax.ShapeDtypeStruct((X, Z) + shape, BF16) for shape in shapes],
        scratch_shapes=[
            pltpu.VMEM((Z, rows, width // Z), BF16),
            pltpu.VMEM((rows, heads), BF16),
            pltpu.VMEM((heads, rows), BF16),
        ]
        + [pltpu.VMEM((Z, X) + shape, BF16) for shape in shapes]
        + [pltpu.SemaphoreType.DMA((4, Z + 1))],
        compiler_params=pltpu.CompilerParams(vmem_limit_bytes=VMEM_LIMIT),
        cost_estimate=pl.CostEstimate(
            flops=2 * rows * width * heads,
            bytes_accessed=2 * width * (rows + heads),
            transcendentals=0,
        ),
    )(place, tokens, cot)


def product_kernel(
    place, tokens, cot, weight_a, weight_c, other_c, keys, back,
    columns, cot_rows, a, c, other, backs, total, sems
):
    part = c.shape[2]
    width = columns.shape[2]
    load = pltpu.make_async_copy(cot, cot_rows, sems.at[0, Z])
    load.start()
    loads = []
    for j in range(Z):
        moves = (
            (weight_a.at[j], a.at[j]),
            (weight_c.at[j], c.at[j]),
            (other_c.at[j], other.at[j]),
            (tokens.at[:, j * width : (j + 1) * width], columns.at[j]),
        )
        loads.append(
            [pltpu.make_async_copy(*move, sems.at[i, j]) for i, move in enumerate(moves)]
        )
        for move in loads[j]:
            move.start()
    load.wait()
    first = place[2] == 0
    stores = []
    for j in range(Z):
        for move in loads[j]:
            move.wait()
        added = None
        for k in range(X):
            block = slice(k * Y * part, (k + 1) * Y * part)
            at = lax.rem(k - place[1] + X, X)
            mine, theirs = c[j, at], other[j, at]
            lower, upper = jnp.where(first, mine, theirs), jnp.where(first, theirs, mine)
            weight = jnp.concatenate([a[j, at], jnp.concatenate([lower, upper])], axis=1)
            product = jnp.dot(columns[j, :, block], weight, preferred_element_type=F32)
            added = product if added is None else added + product
            backs[j, :, block] = lax.dot_general(
                cot_rows[...], weight, (((1,), (1,)), ((), ())), preferred_element_type=F32
            ).astype(BF16)
        if j == 0:
            total[...] = added
        elif j < Z - 1:
            total[...] += added
        else:
            keys[...] = (total[...] + added).astype(BF16)
        stores.append(
            pltpu.make_async_copy(
                backs.at[j], back.at[:, j * width : (j + 1) * width], sems.at[4, j]
            )
        )
        stores[j].start()
    for store in stores:
        store.wait()


def products(place, tokens, cot, weight_a, weight_c, other_c):
    rows, width = tokens.shape
    heads = cot.shape[1]
    anywhere = pl.BlockSpec(memory_space=pl.ANY)
    return pl.pallas_call(
        product_kernel,
        in_specs=[pl.BlockSpec(memory_space=pltpu.SMEM)] + [anywhere] * 5,
        out_specs=[pl.BlockSpec(memory_space=pltpu.VMEM), anywhere],
        scratch_shapes=[
            pltpu.VMEM((Z, rows, width // Z), BF16),
            pltpu.VMEM((rows, heads), BF16),
            pltpu.VMEM(weight_a.shape, BF16),
            pltpu.VMEM(weight_c.shape, BF16),
            pltpu.VMEM(weight_c.shape, BF16),
            pltpu.VMEM((Z, rows, width // Z), BF16),
            pltpu.VMEM((rows, heads), F32),
            pltpu.SemaphoreType.DMA((5, Z + 1)),
        ],
        out_shape=[
            jax.ShapeDtypeStruct((rows, heads), BF16),
            jax.ShapeDtypeStruct((rows, width), BF16),
        ],
        compiler_params=pltpu.CompilerParams(vmem_limit_bytes=VMEM_LIMIT),
        cost_estimate=pl.CostEstimate(
            flops=4 * rows * width * heads,
            bytes_accessed=4 * width * (rows + heads // 2),
            transcendentals=0,
        ),
    )(place, tokens, cot, weight_a, weight_c, other_c)


def gather_x(block):
    return jnp.stack([block] + [shift(block, "x", -k) for k in range(1, X)])


def local(
    tokens, cotangent, key_weight, quant_codes, zero_points, minima, quant_steps, momentum, params
):
    tokens, cot, weight = tokens[0], cotangent[0], key_weight[0]
    rows, width = tokens.shape
    part = weight.shape[0]
    scaling = 1.0 / math.sqrt(rows * Z * X * Y)
    z, x, y = lax.axis_index("z"), lax.axis_index("x"), lax.axis_index("yl")
    place = jnp.stack([z, x, y]).astype(jnp.int32)

    lower = weight[:, :WEIGHT_SPLIT]
    upper = shift(lower, "yl", 1)
    weight_c = gather_x(weight[:, WEIGHT_SPLIT:])
    weight_c, upper = lax.optimization_barrier((weight_c, upper))
    place = after(place, weight_c)
    weight_c = lax.all_gather(weight_c, "z")
    grad_a, keep, send = gradients(place, tokens, cot, part)

    grad_a = lax.psum_scatter(grad_a, "x", scatter_dimension=0, tiled=True)[0]
    got = shift(send, "yl", 1)
    upper = after(upper, send)
    weight_a = jnp.concatenate(
        [jnp.where(y == 0, lower, upper), jnp.where(y == 0, upper, lower)], axis=0
    )
    weight_a = gather_x(weight_a)

    got = after(got, weight_a)
    grad_c = (keep.astype(F32) + got.astype(F32)).astype(BF16)
    grad_c_x = lax.psum_scatter(grad_c, "x", scatter_dimension=0, tiled=True)[0]

    weight_c = after(weight_c, grad_c)
    weight_a = lax.all_gather(after(weight_a, weight_c), "z")
    other_c = shift(weight_c, "yl", 1)

    quant_codes = after(quant_codes[0], weight_c)
    exchanged = outer_values(quant_codes, zero_points[0], minima[0], quant_steps[0])
    new_momentum, new_params = outer_step(exchanged, momentum, params)

    grad_a = after(grad_a, new_params)
    half = GRAD_SPLIT // 2
    at = grad_a.astype(F32)
    up, down = shift(grad_a[4][:half], "z", 1), shift(grad_a[4][half:], "z", -1)
    up = jnp.concatenate([at[3][:half] + up.astype(F32), at[3][half:]]).astype(BF16)
    down = jnp.concatenate([at[5][:half], at[5][half:] + down.astype(F32)]).astype(BF16)
    up, down = lax.optimization_barrier((up, down))
    up, down = shift(up, "z", 1), shift(down, "z", -1)
    up, down = (at[2] + up.astype(F32)).astype(BF16), (at[6] + down.astype(F32)).astype(BF16)
    up, down = lax.optimization_barrier((up, down))
    up, down = shift(up, "z", 1), shift(down, "z", -1)
    up, down = (at[1] + up.astype(F32)).astype(BF16), (at[7] + down.astype(F32)).astype(BF16)
    up, down = lax.optimization_barrier((up, down))
    grad_c = lax.all_to_all(after(grad_c_x, up, other_c), "z", 0, 0, tiled=True)
    up, down = shift(up, "z", 1), shift(down, "z", -1)
    grad_a = at[0] + (up.astype(F32) + down.astype(F32))
    lower, upper = grad_a[:, :part], grad_a[:, part:]
    theirs = jnp.where(y == 0, upper, lower).astype(BF16)
    mine = jnp.where(y == 0, lower, upper)
    weight_a = after(weight_a, theirs)
    grad_a = mine + shift(theirs, "yl", 1).astype(F32)
    grad_c = jnp.sum(grad_c.astype(F32), axis=0)
    weight_grad = jnp.concatenate([grad_a, grad_c]).T * scaling

    keys, back = products(place, tokens, cot, weight_a, weight_c, other_c)
    return keys[None], back[None], weight_grad[None], new_momentum, new_params


def solution(mesh):
    fine = Mesh(mesh.devices.reshape(2, 2, Z, X, Y), ("yh", "c", "z", "x", "yl"))
    island, fsdp = ("yh", "c"), ("z", "x", "yl")
    whole = P(island, fsdp, None)
    return jax.shard_map(
        local,
        mesh=fine,
        in_specs=(whole,) * 7 + (P(fsdp, None),) * 2,
        out_specs=(whole,) * 3 + (P(fsdp, None),) * 2,
        check_vma=False,
    )
```

```python
import math

import jax
import jax.numpy as jnp
from jax import lax
from jax.experimental import pallas as pl
from jax.experimental.pallas import tpu as pltpu
from jax.sharding import Mesh
from jax.sharding import PartitionSpec as P

GROUP = 128
Z, X, Y = 8, 4, 2
WEIGHT_SPLIT = 256
GRAD_SPLIT = 352
F32, BF16 = jnp.float32, jnp.bfloat16
VMEM_LIMIT = 56 * 1024 * 1024


def dequantize(quant_codes, zero_points, minima, quant_steps):
    shape = quant_codes.shape
    grouped = quant_codes.reshape(shape[:-1] + (shape[-1] // GROUP, GROUP))
    offset = (grouped - zero_points[..., None]).astype(F32)
    values = quant_steps[..., None] * offset + minima[..., None]
    return values.reshape(shape)


def shift(block, axis, by):
    size = lax.axis_size(axis)
    return lax.ppermute(block, axis, [(i, (i + by) % size) for i in range(size)])


def after(value, *earlier):
    return lax.optimization_barrier((value, *earlier))[0]


def outer_values(quant_codes, zero_points, minima, quant_steps):
    values = dequantize(quant_codes, zero_points, minima, quant_steps).astype(BF16)
    core = shift(values, "c", 1)
    far = shift(values, "yh", 1)
    far_core = lax.ppermute(values, ("yh", "c"), [(i, 3 - i) for i in range(4)])
    return values, core, far, far_core


def outer_step(exchanged, momentum, params):
    values, core, far, far_core = (v.astype(F32) for v in exchanged)
    delta = ((values + core) + (far + far_core)) / 4
    new_momentum = 0.9 * momentum + delta
    new_params = params - 0.7 * (delta + 0.9 * new_momentum)
    return new_momentum, new_params


def grad_kernel(
    place, tokens, cot, grad_a, keep, send, columns, cot_rows, cot_turned, a, kept, sent, sems
):
    part = kept.shape[3]
    load = pltpu.make_async_copy(cot, cot_rows, sems.at[0, Z])
    load.start()
    loads = []
    for j in range(Z):
        width = columns.shape[2]
        at = pl.multiple_of(lax.rem(place[0] + j, Z) * width, width)
        loads.append(
            pltpu.make_async_copy(tokens.at[:, pl.ds(at, width)], columns.at[j], sems.at[0, j])
        )
        loads[j].start()
    load.wait()
    cot_turned[...] = cot_rows[...].T
    first = place[2] == 0
    stores = []
    for j in range(Z):
        loads[j].wait()
        for k in range(X):
            grad = jnp.dot(
                cot_turned[...],
                columns[j, :, k * Y * part : (k + 1) * Y * part],
                preferred_element_type=F32,
            ).astype(BF16)
            a[j, k] = grad[:GRAD_SPLIT]
            lower, upper = grad[GRAD_SPLIT:, :part], grad[GRAD_SPLIT:, part:]
            kept[j, k] = jnp.where(first, lower, upper)
            sent[j, k] = jnp.where(first, upper, lower)
        own = lax.rem(place[0] + j, Z)
        for i, (buffer, out, to) in enumerate(((a, grad_a, j), (kept, keep, own), (sent, send, own))):
            store = pltpu.make_async_copy(buffer.at[j], out.at[:, to], sems.at[1 + i, j])
            store.start()
            stores.append(store)
    for store in stores:
        store.wait()


def gradients(place, tokens, cot, part):
    rows, width = tokens.shape
    heads = cot.shape[1]
    anywhere = pl.BlockSpec(memory_space=pl.ANY)
    shapes = [(GRAD_SPLIT, Y * part), (heads - GRAD_SPLIT, part), (heads - GRAD_SPLIT, part)]
    return pl.pallas_call(
        grad_kernel,
        in_specs=[pl.BlockSpec(memory_space=pltpu.SMEM), anywhere, anywhere],
        out_specs=[anywhere] * 3,
        out_shape=[jax.ShapeDtypeStruct((X, Z) + shape, BF16) for shape in shapes],
        scratch_shapes=[
            pltpu.VMEM((Z, rows, width // Z), BF16),
            pltpu.VMEM((rows, heads), BF16),
            pltpu.VMEM((heads, rows), BF16),
        ]
        + [pltpu.VMEM((Z, X) + shape, BF16) for shape in shapes]
        + [pltpu.SemaphoreType.DMA((4, Z + 1))],
        compiler_params=pltpu.CompilerParams(vmem_limit_bytes=VMEM_LIMIT),
        cost_estimate=pl.CostEstimate(
            flops=2 * rows * width * heads,
            bytes_accessed=2 * width * (rows + heads),
            transcendentals=0,
        ),
    )(place, tokens, cot)


def product_kernel(
    place, tokens, cot, weight_a, weight_c, other_c, keys, back,
    columns, cot_rows, a, c, other, backs, total, sems
):
    part = c.shape[2]
    width = columns.shape[2]
    load = pltpu.make_async_copy(cot, cot_rows, sems.at[0, Z])
    load.start()
    loads = []
    for j in range(Z):
        moves = (
            (weight_a.at[j], a.at[j]),
            (weight_c.at[j], c.at[j]),
            (other_c.at[j], other.at[j]),
            (tokens.at[:, j * width : (j + 1) * width], columns.at[j]),
        )
        loads.append(
            [pltpu.make_async_copy(*move, sems.at[i, j]) for i, move in enumerate(moves)]
        )
        for move in loads[j]:
            move.start()
    load.wait()
    first = place[2] == 0
    stores = []
    for j in range(Z):
        for move in loads[j]:
            move.wait()
        added = None
        for k in range(X):
            block = slice(k * Y * part, (k + 1) * Y * part)
            at = lax.rem(k - place[1] + X, X)
            mine, theirs = c[j, at], other[j, at]
            lower, upper = jnp.where(first, mine, theirs), jnp.where(first, theirs, mine)
            weight = jnp.concatenate([a[j, at], jnp.concatenate([lower, upper])], axis=1)
            product = jnp.dot(columns[j, :, block], weight, preferred_element_type=F32)
            added = product if added is None else added + product
            backs[j, :, block] = lax.dot_general(
                cot_rows[...], weight, (((1,), (1,)), ((), ())), preferred_element_type=F32
            ).astype(BF16)
        if j == 0:
            total[...] = added
        elif j < Z - 1:
            total[...] += added
        else:
            keys[...] = (total[...] + added).astype(BF16)
        stores.append(
            pltpu.make_async_copy(
                backs.at[j], back.at[:, j * width : (j + 1) * width], sems.at[4, j]
            )
        )
        stores[j].start()
    for store in stores:
        store.wait()


def products(place, tokens, cot, weight_a, weight_c, other_c):
    rows, width = tokens.shape
    heads = cot.shape[1]
    anywhere = pl.BlockSpec(memory_space=pl.ANY)
    return pl.pallas_call(
        product_kernel,
        in_specs=[pl.BlockSpec(memory_space=pltpu.SMEM)] + [anywhere] * 5,
        out_specs=[pl.BlockSpec(memory_space=pltpu.VMEM), anywhere],
        scratch_shapes=[
            pltpu.VMEM((Z, rows, width // Z), BF16),
            pltpu.VMEM((rows, heads), BF16),
            pltpu.VMEM(weight_a.shape, BF16),
            pltpu.VMEM(weight_c.shape, BF16),
            pltpu.VMEM(weight_c.shape, BF16),
            pltpu.VMEM((Z, rows, width // Z), BF16),
            pltpu.VMEM((rows, heads), F32),
            pltpu.SemaphoreType.DMA((5, Z + 1)),
        ],
        out_shape=[
            jax.ShapeDtypeStruct((rows, heads), BF16),
            jax.ShapeDtypeStruct((rows, width), BF16),
        ],
        compiler_params=pltpu.CompilerParams(vmem_limit_bytes=VMEM_LIMIT),
        cost_estimate=pl.CostEstimate(
            flops=4 * rows * width * heads,
            bytes_accessed=4 * width * (rows + heads // 2),
            transcendentals=0,
        ),
    )(place, tokens, cot, weight_a, weight_c, other_c)


def gather_x(block):
    return jnp.stack([block] + [shift(block, "x", -k) for k in range(1, X)])


def local(
    tokens, cotangent, key_weight, quant_codes, zero_points, minima, quant_steps, momentum, params
):
    tokens, cot, weight = tokens[0], cotangent[0], key_weight[0]
    rows, width = tokens.shape
    part = weight.shape[0]
    scaling = 1.0 / math.sqrt(rows * Z * X * Y)
    z, x, y = lax.axis_index("z"), lax.axis_index("x"), lax.axis_index("yl")
    place = jnp.stack([z, x, y]).astype(jnp.int32)

    lower = weight[:, :WEIGHT_SPLIT]
    upper = shift(lower, "yl", 1)
    weight_c = gather_x(weight[:, WEIGHT_SPLIT:])
    weight_c, upper = lax.optimization_barrier((weight_c, upper))
    place = after(place, weight_c)
    weight_c = lax.all_gather(weight_c, "z")
    grad_a, keep, send = gradients(place, tokens, cot, part)

    grad_a = lax.psum_scatter(grad_a, "x", scatter_dimension=0, tiled=True)[0]
    got = shift(send, "yl", 1)
    upper = after(upper, send)
    weight_a = jnp.concatenate(
        [jnp.where(y == 0, lower, upper), jnp.where(y == 0, upper, lower)], axis=0
    )
    weight_a = gather_x(weight_a)

    got = after(got, weight_a)
    grad_c = (keep.astype(F32) + got.astype(F32)).astype(BF16)
    grad_c_x = lax.psum_scatter(grad_c, "x", scatter_dimension=0, tiled=True)[0]

    weight_c = after(weight_c, grad_c)
    weight_a = lax.all_gather(after(weight_a, weight_c), "z")
    other_c = shift(weight_c, "yl", 1)

    quant_codes = after(quant_codes[0], weight_c)
    exchanged = outer_values(quant_codes, zero_points[0], minima[0], quant_steps[0])
    new_momentum, new_params = outer_step(exchanged, momentum, params)

    grad_a = after(grad_a, new_params)
    half = GRAD_SPLIT // 2
    at = grad_a.astype(F32)
    up, down = shift(grad_a[4][:half], "z", 1), shift(grad_a[4][half:], "z", -1)
    up = jnp.concatenate([at[3][:half] + up.astype(F32), at[3][half:]]).astype(BF16)
    down = jnp.concatenate([at[5][:half], at[5][half:] + down.astype(F32)]).astype(BF16)
    up, down = lax.optimization_barrier((up, down))
    up, down = shift(up, "z", 1), shift(down, "z", -1)
    up, down = (at[2] + up.astype(F32)).astype(BF16), (at[6] + down.astype(F32)).astype(BF16)
    up, down = lax.optimization_barrier((up, down))
    up, down = shift(up, "z", 1), shift(down, "z", -1)
    up, down = (at[1] + up.astype(F32)).astype(BF16), (at[7] + down.astype(F32)).astype(BF16)
    up, down = lax.optimization_barrier((up, down))
    grad_c = lax.all_to_all(after(grad_c_x, up, other_c), "z", 0, 0, tiled=True)
    up, down = shift(up, "z", 1), shift(down, "z", -1)
    grad_a = at[0] + (up.astype(F32) + down.astype(F32))
    lower, upper = grad_a[:, :part], grad_a[:, part:]
    theirs = jnp.where(y == 0, upper, lower).astype(BF16)
    mine = jnp.where(y == 0, lower, upper)
    weight_a = after(weight_a, theirs)
    grad_a = mine + shift(theirs, "yl", 1).astype(F32)
    grad_c = jnp.sum(grad_c.astype(F32), axis=0)
    weight_grad = jnp.concatenate([grad_a, grad_c]).T * scaling

    keys, back = products(place, tokens, cot, weight_a, weight_c, other_c)
    return keys[None], back[None], weight_grad[None], new_momentum, new_params


def solution(mesh):
    fine = Mesh(mesh.devices.reshape(2, 2, Z, X, Y), ("yh", "c", "z", "x", "yl"))
    island, fsdp = ("yh", "c"), ("z", "x", "yl")
    whole = P(island, fsdp, None)
    return jax.shard_map(
        local,
        mesh=fine,
        in_specs=(whole,) * 7 + (P(fsdp, None),) * 2,
        out_specs=(whole,) * 3 + (P(fsdp, None),) * 2,
        check_vma=False,
    )
```

```python
import math

import jax
import jax.numpy as jnp
from jax import lax
from jax.experimental import pallas as pl
from jax.experimental.pallas import tpu as pltpu
from jax.sharding import Mesh
from jax.sharding import PartitionSpec as P

GROUP = 128
Z, X, Y = 8, 4, 2
WEIGHT_SPLIT = 256
GRAD_SPLIT = 336
F32, BF16 = jnp.float32, jnp.bfloat16
VMEM_LIMIT = 56 * 1024 * 1024


def dequantize(quant_codes, zero_points, minima, quant_steps):
    shape = quant_codes.shape
    grouped = quant_codes.reshape(shape[:-1] + (shape[-1] // GROUP, GROUP))
    offset = (grouped - zero_points[..., None]).astype(F32)
    values = quant_steps[..., None] * offset + minima[..., None]
    return values.reshape(shape)


def shift(block, axis, by):
    size = lax.axis_size(axis)
    return lax.ppermute(block, axis, [(i, (i + by) % size) for i in range(size)])


def after(value, *earlier):
    return lax.optimization_barrier((value, *earlier))[0]


def outer_values(quant_codes, zero_points, minima, quant_steps):
    values = dequantize(quant_codes, zero_points, minima, quant_steps).astype(BF16)
    core = shift(values, "c", 1)
    far = shift(values, "yh", 1)
    far_core = lax.ppermute(values, ("yh", "c"), [(i, 3 - i) for i in range(4)])
    return values, core, far, far_core


def outer_step(exchanged, momentum, params):
    values, core, far, far_core = (v.astype(F32) for v in exchanged)
    delta = ((values + core) + (far + far_core)) / 4
    new_momentum = 0.9 * momentum + delta
    new_params = params - 0.7 * (delta + 0.9 * new_momentum)
    return new_momentum, new_params


def grad_kernel(
    place, tokens, cot, grad_a, keep, send, columns, cot_rows, cot_turned, a, kept, sent, sems
):
    part = kept.shape[3]
    load = pltpu.make_async_copy(cot, cot_rows, sems.at[0, Z])
    load.start()
    loads = []
    for j in range(Z):
        width = columns.shape[2]
        at = pl.multiple_of(lax.rem(place[0] + j, Z) * width, width)
        loads.append(
            pltpu.make_async_copy(tokens.at[:, pl.ds(at, width)], columns.at[j], sems.at[0, j])
        )
        loads[j].start()
    load.wait()
    cot_turned[...] = cot_rows[...].T
    first = place[2] == 0
    stores = []
    for j in range(Z):
        loads[j].wait()
        for k in range(X):
            grad = jnp.dot(
                cot_turned[...],
                columns[j, :, k * Y * part : (k + 1) * Y * part],
                preferred_element_type=F32,
            ).astype(BF16)
            a[j, k] = grad[:GRAD_SPLIT]
            lower, upper = grad[GRAD_SPLIT:, :part], grad[GRAD_SPLIT:, part:]
            kept[j, k] = jnp.where(first, lower, upper)
            sent[j, k] = jnp.where(first, upper, lower)
        own = lax.rem(place[0] + j, Z)
        for i, (buffer, out, to) in enumerate(((a, grad_a, j), (kept, keep, own), (sent, send, own))):
            store = pltpu.make_async_copy(buffer.at[j], out.at[:, to], sems.at[1 + i, j])
            store.start()
            stores.append(store)
    for store in stores:
        store.wait()


def gradients(place, tokens, cot, part):
    rows, width = tokens.shape
    heads = cot.shape[1]
    anywhere = pl.BlockSpec(memory_space=pl.ANY)
    shapes = [(GRAD_SPLIT, Y * part), (heads - GRAD_SPLIT, part), (heads - GRAD_SPLIT, part)]
    return pl.pallas_call(
        grad_kernel,
        in_specs=[pl.BlockSpec(memory_space=pltpu.SMEM), anywhere, anywhere],
        out_specs=[anywhere] * 3,
        out_shape=[jax.ShapeDtypeStruct((X, Z) + shape, BF16) for shape in shapes],
        scratch_shapes=[
            pltpu.VMEM((Z, rows, width // Z), BF16),
            pltpu.VMEM((rows, heads), BF16),
            pltpu.VMEM((heads, rows), BF16),
        ]
        + [pltpu.VMEM((Z, X) + shape, BF16) for shape in shapes]
        + [pltpu.SemaphoreType.DMA((4, Z + 1))],
        compiler_params=pltpu.CompilerParams(vmem_limit_bytes=VMEM_LIMIT),
        cost_estimate=pl.CostEstimate(
            flops=2 * rows * width * heads,
            bytes_accessed=2 * width * (rows + heads),
            transcendentals=0,
        ),
    )(place, tokens, cot)


def product_kernel(
    place, tokens, cot, weight_a, weight_c, other_c, keys, back,
    columns, cot_rows, a, c, other, backs, total, sems
):
    part = c.shape[2]
    width = columns.shape[2]
    load = pltpu.make_async_copy(cot, cot_rows, sems.at[0, Z])
    load.start()
    loads = []
    for j in range(Z):
        moves = (
            (weight_a.at[j], a.at[j]),
            (weight_c.at[j], c.at[j]),
            (other_c.at[j], other.at[j]),
            (tokens.at[:, j * width : (j + 1) * width], columns.at[j]),
        )
        loads.append(
            [pltpu.make_async_copy(*move, sems.at[i, j]) for i, move in enumerate(moves)]
        )
        for move in loads[j]:
            move.start()
    load.wait()
    first = place[2] == 0
    stores = []
    for j in range(Z):
        for move in loads[j]:
            move.wait()
        added = None
        for k in range(X):
            block = slice(k * Y * part, (k + 1) * Y * part)
            at = lax.rem(k - place[1] + X, X)
            mine, theirs = c[j, at], other[j, at]
            lower, upper = jnp.where(first, mine, theirs), jnp.where(first, theirs, mine)
            weight = jnp.concatenate([a[j, at], jnp.concatenate([lower, upper])], axis=1)
            product = jnp.dot(columns[j, :, block], weight, preferred_element_type=F32)
            added = product if added is None else added + product
            backs[j, :, block] = lax.dot_general(
                cot_rows[...], weight, (((1,), (1,)), ((), ())), preferred_element_type=F32
            ).astype(BF16)
        if j == 0:
            total[...] = added
        elif j < Z - 1:
            total[...] += added
        else:
            keys[...] = (total[...] + added).astype(BF16)
        stores.append(
            pltpu.make_async_copy(
                backs.at[j], back.at[:, j * width : (j + 1) * width], sems.at[4, j]
            )
        )
        stores[j].start()
    for store in stores:
        store.wait()


def products(place, tokens, cot, weight_a, weight_c, other_c):
    rows, width = tokens.shape
    heads = cot.shape[1]
    anywhere = pl.BlockSpec(memory_space=pl.ANY)
    return pl.pallas_call(
        product_kernel,
        in_specs=[pl.BlockSpec(memory_space=pltpu.SMEM)] + [anywhere] * 5,
        out_specs=[pl.BlockSpec(memory_space=pltpu.VMEM), anywhere],
        scratch_shapes=[
            pltpu.VMEM((Z, rows, width // Z), BF16),
            pltpu.VMEM((rows, heads), BF16),
            pltpu.VMEM(weight_a.shape, BF16),
            pltpu.VMEM(weight_c.shape, BF16),
            pltpu.VMEM(weight_c.shape, BF16),
            pltpu.VMEM((Z, rows, width // Z), BF16),
            pltpu.VMEM((rows, heads), F32),
            pltpu.SemaphoreType.DMA((5, Z + 1)),
        ],
        out_shape=[
            jax.ShapeDtypeStruct((rows, heads), BF16),
            jax.ShapeDtypeStruct((rows, width), BF16),
        ],
        compiler_params=pltpu.CompilerParams(vmem_limit_bytes=VMEM_LIMIT),
        cost_estimate=pl.CostEstimate(
            flops=4 * rows * width * heads,
            bytes_accessed=4 * width * (rows + heads // 2),
            transcendentals=0,
        ),
    )(place, tokens, cot, weight_a, weight_c, other_c)


def gather_x(block):
    return jnp.stack([block] + [shift(block, "x", -k) for k in range(1, X)])


def local(
    tokens, cotangent, key_weight, quant_codes, zero_points, minima, quant_steps, momentum, params
):
    tokens, cot, weight = tokens[0], cotangent[0], key_weight[0]
    rows, width = tokens.shape
    part = weight.shape[0]
    scaling = 1.0 / math.sqrt(rows * Z * X * Y)
    z, x, y = lax.axis_index("z"), lax.axis_index("x"), lax.axis_index("yl")
    place = jnp.stack([z, x, y]).astype(jnp.int32)

    lower = weight[:, :WEIGHT_SPLIT]
    upper = shift(lower, "yl", 1)
    weight_c = gather_x(weight[:, WEIGHT_SPLIT:])
    weight_c, upper = lax.optimization_barrier((weight_c, upper))
    place = after(place, weight_c)
    weight_c = lax.all_gather(weight_c, "z")
    grad_a, keep, send = gradients(place, tokens, cot, part)

    grad_a = lax.psum_scatter(grad_a, "x", scatter_dimension=0, tiled=True)[0]
    got = shift(send, "yl", 1)
    upper = after(upper, send)
    weight_a = jnp.concatenate(
        [jnp.where(y == 0, lower, upper), jnp.where(y == 0, upper, lower)], axis=0
    )
    weight_a = gather_x(weight_a)

    got = after(got, weight_a)
    grad_c = (keep.astype(F32) + got.astype(F32)).astype(BF16)
    grad_c_x = lax.psum_scatter(grad_c, "x", scatter_dimension=0, tiled=True)[0]

    weight_c = after(weight_c, grad_c)
    weight_a = lax.all_gather(after(weight_a, weight_c), "z")
    other_c = shift(weight_c, "yl", 1)

    quant_codes = after(quant_codes[0], weight_c)
    exchanged = outer_values(quant_codes, zero_points[0], minima[0], quant_steps[0])
    new_momentum, new_params = outer_step(exchanged, momentum, params)

    grad_a = after(grad_a, new_params)
    half = GRAD_SPLIT // 32 * 16
    at = grad_a.astype(F32)
    up, down = shift(grad_a[4][:half], "z", 1), shift(grad_a[4][half:], "z", -1)
    up = jnp.concatenate([at[3][:half] + up.astype(F32), at[3][half:]]).astype(BF16)
    down = jnp.concatenate([at[5][:half], at[5][half:] + down.astype(F32)]).astype(BF16)
    up, down = lax.optimization_barrier((up, down))
    up, down = shift(up, "z", 1), shift(down, "z", -1)
    up, down = (at[2] + up.astype(F32)).astype(BF16), (at[6] + down.astype(F32)).astype(BF16)
    up, down = lax.optimization_barrier((up, down))
    up, down = shift(up, "z", 1), shift(down, "z", -1)
    up, down = (at[1] + up.astype(F32)).astype(BF16), (at[7] + down.astype(F32)).astype(BF16)
    up, down = lax.optimization_barrier((up, down))
    grad_c = lax.all_to_all(after(grad_c_x, up, other_c), "z", 0, 0, tiled=True)
    up, down = shift(up, "z", 1), shift(down, "z", -1)
    grad_a = at[0] + (up.astype(F32) + down.astype(F32))
    lower, upper = grad_a[:, :part], grad_a[:, part:]
    theirs = jnp.where(y == 0, upper, lower).astype(BF16)
    mine = jnp.where(y == 0, lower, upper)
    weight_a = after(weight_a, theirs)
    grad_a = mine + shift(theirs, "yl", 1).astype(F32)
    grad_c = jnp.sum(grad_c.astype(F32), axis=0)
    weight_grad = jnp.concatenate([grad_a, grad_c]).T * scaling

    keys, back = products(place, tokens, cot, weight_a, weight_c, other_c)
    return keys[None], back[None], weight_grad[None], new_momentum, new_params


def solution(mesh):
    fine = Mesh(mesh.devices.reshape(2, 2, Z, X, Y), ("yh", "c", "z", "x", "yl"))
    island, fsdp = ("yh", "c"), ("z", "x", "yl")
    whole = P(island, fsdp, None)
    return jax.shard_map(
        local,
        mesh=fine,
        in_specs=(whole,) * 7 + (P(fsdp, None),) * 2,
        out_specs=(whole,) * 3 + (P(fsdp, None),) * 2,
        check_vma=False,
    )
```
